128 devices in a mesh: row: 8 (over z, core), col: 16 (over x, y).
Axes of the slice: x: 4, y: 4, z: 4, core: 2. Of those that a mesh axis runs over, the one named last changes fastest.
Arguments:
- rhs: float32 [128, 128, 384], P('row', 'col'), may hold values from -10 to 10
- storage: float32 [128, 128, 384], P('row', 'col'), may hold values from 0.02 to 0.5
- class_id: int32 [128, 128, 96], P('row', 'col'), may hold values from 0 to 7
- class_conductivity: float32 [8], replicated, may hold values from 0.2 to 5
- basis: bfloat16 [64, 128, 128, 384], P(None, 'row', 'col'), may hold values from -1 to 1
Outputs:
- solution: float32 [128, 128, 384], P('row', 'col')
- residual: float32 [128, 128, 384], P('row', 'col')
The draws below stay inside these ranges and needn't reach their ends.
All inputs are finite; a program needn't handle non-finite values.
Results may differ from the reference program's by a relative error of at most 0.0091.
Values may be sent and summed in bfloat16 or wider, within the bound.
No kernel may reach another device: no remote copies, remote signals or barrier semaphores. Data moves between devices by JAX's collectives and lax.ppermute only.
A program may use at most 192 MiB of HBM per device.

```python
import math
from functools import partial
import jax
import jax.numpy as jnp
from jax import lax

K = 64
CLASSES = 8
TILE = 4
CX = 16
CY = 8
NZ = 384
ITERS = 2
SWEEPS = 4
NX = 128
NY = 128
N_ROW = 8
N_COL = 16


def draw_basis(key, part):
    key = jax.random.fold_in(key, 7)
    amp_key, noise_key = jax.random.split(key)
    vector_ids = jnp.arange(K)
    order_x = (vector_ids % 4).astype(jnp.float32)
    order_y = (vector_ids // 4 % 4).astype(jnp.float32)
    order_z = (vector_ids // 16).astype(jnp.float32)
    coord_x = ((jnp.arange(NX) % CX).astype(jnp.float32) + 0.5) / CX
    coord_y = ((jnp.arange(NY) % CY).astype(jnp.float32) + 0.5) / CY
    coord_z = (jnp.arange(NZ).astype(jnp.float32) + 0.5) / NZ
    shape_x = jnp.cos(jnp.pi * order_x[:, None] * coord_x[None, :])
    shape_y = jnp.cos(jnp.pi * order_y[:, None] * coord_y[None, :])
    shape_z = jnp.cos(jnp.pi * order_z[:, None] * coord_z[None, :])
    amplitude = jax.random.uniform(amp_key, (K, NX // CX, NY // CY), minval=0.5, maxval=1.5)
    amplitude = jnp.repeat(jnp.repeat(amplitude, CX, axis=1), CY, axis=2)
    smooth = amplitude[..., None] * shape_x[:, :, None, None] * shape_y[:, None, :, None] * shape_z[:, None, None, :]
    noise = 0.08 * jax.random.truncated_normal(noise_key, -3.0, 3.0, (K, NX, NY, NZ))
    return ((smooth + noise) / math.sqrt(CX * CY * NZ)).astype(jnp.bfloat16)


def draw_rhs(key, part):
    key = jax.random.fold_in(key, 11)
    phase_key, noise_key = jax.random.split(key)
    phases = jax.random.uniform(phase_key, (3,), minval=-jnp.pi, maxval=jnp.pi)
    coord_x = (jnp.arange(NX).astype(jnp.float32) + 0.5) / NX
    coord_y = (jnp.arange(NY).astype(jnp.float32) + 0.5) / NY
    coord_z = (jnp.arange(NZ).astype(jnp.float32) + 0.5) / NZ
    wave_x = jnp.cos(2.0 * jnp.pi * coord_x + phases[0])
    wave_y = jnp.cos(2.0 * jnp.pi * coord_y + phases[1])
    wave_z = jnp.cos(jnp.pi * coord_z + phases[2])
    lateral = wave_x[:, None, None] * wave_y[None, :, None]
    vertical = wave_z[None, None, :]
    smooth = 0.5 + 1.5 * lateral + 0.8 * vertical
    noise = jax.random.truncated_normal(noise_key, -4.0, 4.0, (NX, NY, NZ))
    return (smooth + noise).astype(jnp.float32)


def place_ends(drawn, own_key, low, top_value):
    longest = drawn.shape.index(max(drawn.shape))
    spots = []
    for shift in (0, 1):
        where = [jax.random.randint(jax.random.fold_in(own_key, axis), (), 0, length) for axis, length in enumerate(drawn.shape)]
        where[longest] = (where[longest] + shift) % drawn.shape[longest]
        spots.append(tuple(where))
    return drawn.at[spots[0]].set(low).at[spots[1]].set(top_value)


def block_levels(key, extent, cuts, smallest, top_value):
    factor_of = 1.0
    for position, blocks in cuts:
        steps = jax.random.uniform(jax.random.fold_in(jax.random.fold_in(key, 6), position), (blocks,), jnp.float32, smallest / len(cuts), top_value / len(cuts))
        factor_of = factor_of * jnp.repeat(jnp.exp(steps), extent[position] // blocks).reshape((-1,) + (1,) * (len(extent) - 1 - position))
    return factor_of


def setup_inputs(seed: int = 0) -> dict:
    streams_of = jax.random.split(jax.random.key(seed), 6)
    return {
        "rhs": draw_rhs(jax.random.fold_in(streams_of[5], 71), 0),
        "storage": jnp.clip(jnp.exp(math.log(0.5) - 3.218876 * jax.random.uniform(streams_of[1], (NX, NY, NZ), jnp.float32) ** block_levels(streams_of[1], (NX, NY, NZ), ((0, 8), (1, 16)), -0.2, 0.2)), 0.02, 0.5),
        "class_id": place_ends(jax.random.randint(streams_of[2], (NX, NY, NZ // TILE), 0, CLASSES), jax.random.fold_in(streams_of[2], 1), 0, CLASSES - 1).astype(jnp.int32),
        "class_conductivity": jnp.clip(jnp.exp(jax.random.uniform(streams_of[3], (CLASSES,), jnp.float32, math.log(0.2), math.log(5.0))), 0.2, 5.0),
        "basis": draw_basis(jax.random.fold_in(streams_of[5], 71), 0),
    }


relax = 0.8
highest = lax.Precision.HIGHEST

def harmonic(left, right):
    return 2.0 * left * right / (left + right)

def conductances(storage, class_id, class_conductivity):
    labels = jnp.arange(CLASSES, dtype=jnp.int32)
    tiles = jnp.sum(jnp.where(class_id[..., None] == labels, class_conductivity, jnp.float32(0.0)), axis=-1)
    cells = jnp.repeat(tiles, TILE, axis=2)
    padded = jnp.pad(cells, 1)
    faces = (harmonic(cells, padded[:-2, 1:-1, 1:-1]), harmonic(cells, padded[2:, 1:-1, 1:-1]), harmonic(cells, padded[1:-1, :-2, 1:-1]), harmonic(cells, padded[1:-1, 2:, 1:-1]), harmonic(cells, padded[1:-1, 1:-1, :-2]), harmonic(cells, padded[1:-1, 1:-1, 2:]))
    diagonal = storage + faces[0] + faces[1] + faces[2] + faces[3] + faces[4] + faces[5]
    return (faces, diagonal)

def stencil(field, faces, diagonal):
    widths = [(0, 0)] * (field.ndim - 3) + [(1, 1)] * 3
    padded = jnp.pad(field, widths)
    result = diagonal * field
    result = result - faces[0] * padded[..., :-2, 1:-1, 1:-1]
    result = result - faces[1] * padded[..., 2:, 1:-1, 1:-1]
    result = result - faces[2] * padded[..., 1:-1, :-2, 1:-1]
    result = result - faces[3] * padded[..., 1:-1, 2:, 1:-1]
    result = result - faces[4] * padded[..., 1:-1, 1:-1, :-2]
    result = result - faces[5] * padded[..., 1:-1, 1:-1, 2:]
    return result

def invert(block):
    lower = jnp.linalg.cholesky(block)
    identity = jnp.eye(block.shape[-1], dtype=jnp.float32)
    lower_inv = lax.linalg.triangular_solve(lower, identity, left_side=True, lower=True)
    return jnp.dot(lower_inv.T, lower_inv, precision=highest)

def face_block(own_face, weight, neighbour):
    scaled = (weight * own_face).astype(jnp.bfloat16).reshape(K, -1)
    return -lax.dot_general(scaled.astype(jnp.float32), neighbour.reshape(K, -1).astype(jnp.float32), (((1,), (1,)), ((), ())), preferred_element_type=jnp.float32)

def block_coarse(basis, faces, diagonal, block_index):
    anchor = jnp.zeros((), jnp.int32)
    row_index = (block_index // N_COL).astype(jnp.int32)
    col_index = (block_index % N_COL).astype(jnp.int32)
    start_x = row_index * CX
    start_y = col_index * CY
    own = lax.dynamic_slice(basis, (anchor, start_x, start_y, anchor), (K, CX, CY, NZ))
    local_faces = tuple((lax.dynamic_slice(face, (start_x, start_y, anchor), (CX, CY, NZ)) for face in faces))
    local_diag = lax.dynamic_slice(diagonal, (start_x, start_y, anchor), (CX, CY, NZ))
    applied = stencil(own, local_faces, local_diag).astype(jnp.bfloat16)
    galerkin = lax.dot_general(own.reshape(K, -1).astype(jnp.float32), applied.reshape(K, -1).astype(jnp.float32), (((1,), (1,)), ((), ())), preferred_element_type=jnp.float32)
    block_diag = 0.5 * (galerkin + galerkin.T)
    lower_x = jnp.maximum(start_x - 1, 0).astype(jnp.int32)
    upper_x = jnp.minimum(start_x + CX, NX - 1).astype(jnp.int32)
    lower_y = jnp.maximum(start_y - 1, 0).astype(jnp.int32)
    upper_y = jnp.minimum(start_y + CY, NY - 1).astype(jnp.int32)
    minus_x = lax.dynamic_slice(basis, (anchor, lower_x, start_y, anchor), (K, 1, CY, NZ))[:, 0]
    plus_x = lax.dynamic_slice(basis, (anchor, upper_x, start_y, anchor), (K, 1, CY, NZ))[:, 0]
    minus_y = lax.dynamic_slice(basis, (anchor, start_x, lower_y, anchor), (K, CX, 1, NZ))[:, :, 0]
    plus_y = lax.dynamic_slice(basis, (anchor, start_x, upper_y, anchor), (K, CX, 1, NZ))[:, :, 0]
    blocks = jnp.stack([face_block(own[:, 0], local_faces[0][0], minus_x), face_block(own[:, -1], local_faces[1][-1], plus_x), face_block(own[:, :, 0], local_faces[2][:, 0], minus_y), face_block(own[:, :, -1], local_faces[3][:, -1], plus_y)])
    return (block_diag, blocks)

def matvec(matrix, vector):
    return jnp.einsum('abkl,abl->abk', matrix, vector, precision=highest)

def coarse_solve(rhs_coarse, block_diag, inverse, off_blocks):
    iterate = relax * matvec(inverse, rhs_coarse)
    for sweep_index in range(SWEEPS - 1):
        padded = jnp.pad(iterate, ((1, 1), (1, 1), (0, 0)))
        product = matvec(block_diag, iterate)
        product = product + matvec(off_blocks[:, :, 0], padded[:-2, 1:-1])
        product = product + matvec(off_blocks[:, :, 1], padded[2:, 1:-1])
        product = product + matvec(off_blocks[:, :, 2], padded[1:-1, :-2])
        product = product + matvec(off_blocks[:, :, 3], padded[1:-1, 2:])
        iterate = iterate + relax * matvec(inverse, rhs_coarse - product)
    return iterate

def project(basis, field):
    rounded = field.astype(jnp.bfloat16)
    anchor = jnp.zeros((), jnp.int32)

    def single(block_index):
        start_x = (block_index // N_COL).astype(jnp.int32) * CX
        start_y = (block_index % N_COL).astype(jnp.int32) * CY
        part_basis = lax.dynamic_slice(basis, (anchor, start_x, start_y, anchor), (K, CX, CY, NZ))
        part_field = lax.dynamic_slice(rounded, (start_x, start_y, anchor), (CX, CY, NZ))
        return jnp.dot(part_basis.reshape(K, -1).astype(jnp.float32), part_field.reshape(-1).astype(jnp.float32), preferred_element_type=jnp.float32)
    return lax.map(single, jnp.arange(N_ROW * N_COL, dtype=jnp.int32)).reshape(N_ROW, N_COL, K)

def expand(basis, coeffs):
    anchor = jnp.zeros((), jnp.int32)

    def single(block_index):
        row_index = (block_index // N_COL).astype(jnp.int32)
        col_index = (block_index % N_COL).astype(jnp.int32)
        part_basis = lax.dynamic_slice(basis, (anchor, row_index * CX, col_index * CY, anchor), (K, CX, CY, NZ))
        vector = coeffs[row_index, col_index].astype(jnp.bfloat16)
        return jnp.dot(vector.astype(jnp.float32), part_basis.reshape(K, -1).astype(jnp.float32), preferred_element_type=jnp.float32).reshape(CX, CY, NZ)
    pieces = lax.map(single, jnp.arange(N_ROW * N_COL, dtype=jnp.int32)).reshape(N_ROW, N_COL, CX, CY, NZ)
    return pieces.transpose(0, 2, 1, 3, 4).reshape(NX, NY, NZ)

def reference(rhs, storage, class_id, class_conductivity, basis):
    faces, diagonal = conductances(storage, class_id, class_conductivity)
    block_diag, off_blocks = lax.map(partial(block_coarse, basis, faces, diagonal), jnp.arange(N_ROW * N_COL, dtype=jnp.int32))
    inverse = jax.vmap(invert)(block_diag).reshape(N_ROW, N_COL, K, K)
    block_diag = block_diag.reshape(N_ROW, N_COL, K, K)
    off_blocks = off_blocks.reshape(N_ROW, N_COL, 4, K, K)

    def solve(rhs_coarse):
        return coarse_solve(rhs_coarse, block_diag, inverse, off_blocks)
    solution = expand(basis, solve(project(basis, rhs)))
    residual = rhs - stencil(solution, faces, diagonal)
    direction = residual - expand(basis, solve(project(basis, stencil(residual, faces, diagonal))))
    norm_now = jnp.sum(residual * residual)
    for step_index in range(ITERS):
        image = stencil(direction, faces, diagonal)
        alpha = norm_now / jnp.sum(direction * image)
        solution = solution + alpha * direction
        residual = residual - alpha * image
        norm_next = jnp.sum(residual * residual)
        if step_index + 1 < ITERS:
            coeffs = solve(project(basis, stencil(residual, faces, diagonal)))
            direction = norm_next / norm_now * direction + residual - expand(basis, coeffs)
            norm_now = norm_next
    return (solution, residual)
```

```python
import functools

import jax
import jax.numpy as jnp
from jax import lax
from jax.experimental import pallas as pl
from jax.experimental.pallas import tpu as pltpu
from jax.sharding import PartitionSpec as P

K = 64
CX = 16
CY = 8
NZ = 384
TILES = 96
CLASSES = 8
EX = CX + 4
EY = 16
Y0 = 4
REACH = 3
BLOCKS = 8
relax = 0.8
keep = 0.2
highest = lax.Precision.HIGHEST
f32 = jnp.float32
bf16 = jnp.bfloat16
VMEM = pl.BlockSpec(memory_space=pltpu.VMEM)
SMEM = pl.BlockSpec(memory_space=pltpu.SMEM)


def call(kernel, outs, args, scratch=(), smem=0, flops=1000000, limit=48):
    return pl.pallas_call(
        kernel,
        out_shape=[jax.ShapeDtypeStruct(s, d) for s, d in outs],
        in_specs=[SMEM] * smem + [VMEM] * (len(args) - smem),
        out_specs=[VMEM] * len(outs),
        scratch_shapes=list(scratch),
        cost_estimate=pl.CostEstimate(flops=flops, bytes_accessed=4000000, transcendentals=0),
        compiler_params=pltpu.CompilerParams(vmem_limit_bytes=limit << 20),
    )(*args)


def ring(x, axis, shift):
    count = lax.axis_size(axis)
    return lax.ppermute(x, axis, [(i, (i + shift) % count) for i in range(count)])


def gather(payload, axes=("row", "col")):
    count = lax.axis_size(axes)
    return lax.all_to_all(jnp.broadcast_to(payload, (count, payload.shape[-1])), axes, 0, 0)


def harmonic(a, b):
    return 2.0 * a * b / jnp.maximum(a + b, 1e-6)


def lookup(ids, table):
    tiles = jnp.zeros(ids.shape, f32)
    for label in range(CLASSES):
        tiles = jnp.where(ids == label, table[label], tiles)
    tile = lax.broadcasted_iota(jnp.int32, (TILES, NZ), 0)
    cell = lax.broadcasted_iota(jnp.int32, (TILES, NZ), 1)
    spread = jnp.where(lax.shift_right_logical(cell, 2) == tile, 1.0, 0.0)
    return jnp.dot(tiles, spread, precision=highest, preferred_element_type=f32)


def down(v):
    return pltpu.roll(v, v.shape[-2] - 1, v.ndim - 2)


def up(v):
    return pltpu.roll(v, 1, v.ndim - 2)


def fore(v):
    return pltpu.roll(v, NZ - 1, v.ndim - 1)


def back(v):
    return pltpu.roll(v, 1, v.ndim - 1)


def faces_kernel(w_ref, fx_ref, fy_ref):
    source = lax.broadcasted_iota(jnp.int32, (K * CY, K * CY), 1)
    target = lax.broadcasted_iota(jnp.int32, (K * CY, K * CY), 0)
    order = jnp.where(source == (target & (K - 1)) * CY + lax.shift_right_logical(target, 6), 1.0, 0.0).astype(bf16)
    for side, x in ((0, 0), (1, CX - 1)):
        slab = w_ref[:, x].reshape(K * CY, NZ)
        fx_ref[side] = (
            jnp.dot(order, slab, preferred_element_type=f32).astype(bf16).reshape(CY, K, NZ)
        )
    ends = jnp.concatenate([order[:K], order[(CY - 1) * K :]], axis=0)
    for x in range(CX):
        slab = w_ref[:, x].reshape(K * CY, NZ)
        both = jnp.dot(ends, slab, preferred_element_type=f32).astype(bf16)
        fy_ref[0, x] = both[:K]
        fy_ref[1, x] = both[K:]


def galerkin_kernel(table, w_ref, id_ref, s_ref, r_ref, g_ref, p_ref, coef, bs, acc, gp):
    width = 4
    row = lax.broadcasted_iota(jnp.int32, (CY, NZ), 0)
    lane = lax.broadcasted_iota(jnp.int32, (CY, NZ), 1)
    cells = lookup(id_ref[...].reshape(CX * CY, TILES), table).reshape(CX, CY, NZ)
    before = jnp.zeros((CY, NZ), f32)
    for x in range(CX):
        c = cells[x]
        fx = harmonic(c, cells[x + 1]) if x < CX - 1 else jnp.zeros_like(c)
        fy = jnp.where(row < CY - 1, harmonic(c, down(c)), 0.0)
        fz = jnp.where(lane < NZ - 1, harmonic(c, fore(c)), 0.0)
        coef[0, x] = 0.5 * (s_ref[x] + before + fx + up(fy) + fy + back(fz) + fz)
        coef[1, x] = fx
        coef[2, x] = fy
        coef[3, x] = fz
        before = fx
    acc[...] = jnp.zeros_like(acc)
    gp[...] = jnp.zeros_like(gp)

    def block(xb, _):
        for xi in range(width):
            x = xb * width + xi
            xn = jnp.minimum(x + 1, CX - 1)
            half = coef[0, x]
            fx = coef[1, x]
            fy = coef[2, x]
            fz = coef[3, x]
            v = r_ref[x].astype(bf16).astype(f32)
            for k in range(K):
                w = w_ref[k, x].astype(f32)
                b = half * w - fx * w_ref[k, xn].astype(f32) - fy * down(w) - fz * fore(w)
                bs[xi, k] = b.astype(bf16)
                q = w * v
                gp[k] += q[:, :128] + q[:, 128:256] + q[:, 256:]
        total = None
        for xi in range(width):
            part = lax.dot_general(
                w_ref[:, xb * width + xi].reshape(K * CY, NZ),
                bs[xi].reshape(K * CY, NZ),
                (((1,), (1,)), ((), ())),
                preferred_element_type=f32,
            )
            total = part if total is None else total + part
        acc[...] += total
        return 0

    lax.fori_loop(0, CX // width, block, 0)
    ri = lax.broadcasted_iota(jnp.int32, (K * CY, K * CY), 0) & (CY - 1)
    ci = lax.broadcasted_iota(jnp.int32, (K * CY, K * CY), 1) & (CY - 1)
    same = jnp.where(ri == ci, acc[...], 0.0)
    kr = lax.shift_right_logical(lax.broadcasted_iota(jnp.int32, (K * CY, K), 0), 3)
    pick = jnp.where(kr == lax.broadcasted_iota(jnp.int32, (K * CY, K), 1), 1.0, 0.0)
    side = jnp.dot(same, pick, precision=highest, preferred_element_type=f32)
    g = lax.dot_general(pick, side, (((0,), (0,)), ((), ())), precision=highest, preferred_element_type=f32)
    g_ref[...] = g + g.T
    p_ref[...] = jnp.broadcast_to(jnp.sum(jnp.sum(gp[...], axis=1), axis=1, keepdims=True), (K, 128))


def coef_kernel(
    where, table, id_ref, ixm, ixp, iym, iyp, s_ref, sxm, sxp, sym, syp, ofx, ofy, g_ref, p_ref,
    fx_ref, fy_ref, fz_ref, dg_ref, inv_ref, b_ref, cells, stor,
):
    r = where[0]
    c = where[1]
    inside = lambda cond: jnp.where(cond, 1.0, 0.0)
    cells[...] = jnp.zeros_like(cells)
    cells[2 : 2 + CX, Y0 : Y0 + CY] = lookup(id_ref[...].reshape(CX * CY, TILES), table).reshape(CX, CY, NZ)
    low = lookup(ixm[...].reshape(2 * CY, TILES), table).reshape(2, CY, NZ) * inside(r > 0)
    high = lookup(ixp[...].reshape(2 * CY, TILES), table).reshape(2, CY, NZ) * inside(r < where[2] - 1)
    cells[0:2, Y0 : Y0 + CY] = low
    cells[2 + CX :, Y0 : Y0 + CY] = high
    xs = lax.broadcasted_iota(jnp.int32, (EX, NZ), 0)
    ok = jnp.where(xs < 2, inside(r > 0), jnp.where(xs >= CX + 2, inside(r < where[2] - 1), 1.0))
    for j in range(2):
        cells[:, Y0 - 2 + j] = lookup(iym[j], table) * ok * inside(c > 0)
        cells[:, Y0 + CY + j] = lookup(iyp[j], table) * ok * inside(c < where[3] - 1)
    stor[...] = jnp.zeros_like(stor)
    stor[2 : 2 + CX, Y0 : Y0 + CY] = s_ref[...]
    stor[1, Y0 : Y0 + CY] = sxm[0]
    stor[2 + CX, Y0 : Y0 + CY] = sxp[0]
    stor[2 : 2 + CX, Y0 - 1] = sym[...]
    stor[2 : 2 + CX, Y0 + CY] = syp[...]
    lane = lax.broadcasted_iota(jnp.int32, (EY, NZ), 1)
    before = jnp.zeros((EY, NZ), f32)
    for x in range(EX):
        v = cells[x]
        fx = harmonic(v, cells[x + 1]) if x < EX - 1 else jnp.zeros_like(v)
        fy = harmonic(v, down(v))
        fz = jnp.where(lane < NZ - 1, harmonic(v, fore(v)), 0.0)
        dg_ref[x] = stor[x] + before + fx + up(fy) + fy + back(fz) + fz
        fx_ref[x] = fx
        fy_ref[x] = fy
        fz_ref[x] = fz
        before = fx

    total = jnp.zeros((K, K), f32)
    for side, x in ((0, 1), (1, CX + 1)):
        for y in range(CY):
            w = ofx[side, y]
            scaled = (w.astype(f32) * fx_ref[x, pl.ds(Y0 + y, 1)]).astype(bf16)
            total += lax.dot_general(scaled, w, (((1,), (1,)), ((), ())), preferred_element_type=f32)
    for side, y in ((0, Y0 - 1), (1, Y0 + CY - 1)):
        for x in range(CX):
            w = ofy[side, x]
            scaled = (w.astype(f32) * fy_ref[2 + x, pl.ds(y, 1)]).astype(bf16)
            total += lax.dot_general(scaled, w, (((1,), (1,)), ((), ())), preferred_element_type=f32)
    a = g_ref[...] + 0.5 * (total + total.T)

    sub = lax.broadcasted_iota(jnp.int32, (K, K), 0)
    lan = lax.broadcasted_iota(jnp.int32, (K, K), 1)
    lan1 = lax.broadcasted_iota(jnp.int32, (1, K), 1)
    for k in range(K):
        pivot = 1.0 / a[k : k + 1, k : k + 1]
        line = jnp.where(lan1 == k, pivot, a[k : k + 1, :] * pivot)
        a = jnp.where(sub == k, line, jnp.where(lan == k, 0.0, a) - a[:, k : k + 1] * line)
    inv_ref[...] = a
    b_ref[...] = relax * jnp.dot(a, p_ref[...], precision=highest, preferred_element_type=f32)


def couple_kernel(fx_ref, fy_ref, inv_ref, b_ref, ofx, ofy, nxm, nxp, nym, nyp, f_ref, m_ref):
    f_parts = []
    for side, x, other in ((0, 1, nxm), (1, CX + 1, nxp)):
        total = jnp.zeros((K, K), f32)
        for y in range(CY):
            scaled = (ofx[side, y].astype(f32) * fx_ref[x, pl.ds(Y0 + y, 1)]).astype(bf16)
            total += lax.dot_general(scaled, other[y], (((1,), (1,)), ((), ())), preferred_element_type=f32)
        f_parts.append(total)
    for side, y, other in ((0, Y0 - 1, nym), (1, Y0 + CY - 1, nyp)):
        total = jnp.zeros((K, K), f32)
        for x in range(CX):
            scaled = (ofy[side, x].astype(f32) * fy_ref[2 + x, pl.ds(y, 1)]).astype(bf16)
            total += lax.dot_general(scaled, other[x], (((1,), (1,)), ((), ())), preferred_element_type=f32)
        f_parts.append(total)
    inv = inv_ref[...]
    eye = jnp.where(
        lax.broadcasted_iota(jnp.int32, (K, K), 0) == lax.broadcasted_iota(jnp.int32, (K, K), 1), 1.0 + keep, 0.0
    )
    for n in range(4):
        minus = relax * jnp.dot(inv, f_parts[n], precision=highest, preferred_element_type=f32)
        f_ref[n] = minus
        spot = (0, 4, 1, 3)[n]
        m_ref[:, spot * K : spot * K + K] = minus
    m_ref[:, 2 * K : 3 * K] = eye
    m_ref[:, 5 * K : 6 * K] = jnp.zeros((K, K), f32)
    m_ref[:, 6 * K : 8 * K] = b_ref[...]


R1_BLOCKS = ((-1, 0), (0, -1), (0, 0), (0, 1), (1, 0))
R2_BLOCKS = tuple((a, b) for a in range(-2, 3) for b in range(-2, 3) if abs(a) + abs(b) <= 2)
NEIGHBOURS = ((-1, 0), (1, 0), (0, -1), (0, 1))


def spread_kernel(blocks, radius, base_blocks, f_ref, b_ref, own_ref, nxm, nxp, nym, nyp, out_ref, y_ref, held):
    others = (nxm, nxp, nym, nyp)
    wide = -(-len(blocks) // 2) * 2 * K
    held[...] = jnp.zeros_like(held)
    for n, (a0, b0) in enumerate(NEIGHBOURS):
        for i, (a, b) in enumerate(blocks):
            at = (b + b0 + REACH) * K
            held[n, a + a0 + REACH, :, at : at + K] = others[n][:, i * K : i * K + K]
    for i, (a, b) in enumerate(blocks):
        at = (b + REACH) * K
        held[4, a + REACH, :, at : at + K] = own_ref[:, i * K : i * K + K]
    for a in range(-radius, radius + 1):
        total = keep * held[4, a + REACH]
        for n in range(4):
            total += jnp.dot(f_ref[n], held[n, a + REACH], precision=highest, preferred_element_type=f32)
        if a == 0:
            lane = lax.broadcasted_iota(jnp.int32, (K, BLOCKS * K), 1)
            sub = lax.broadcasted_iota(jnp.int32, (K, BLOCKS * K), 0)
            total += jnp.where(lane == sub + REACH * K, 1.0, 0.0)
        held[5, a + REACH] = total
    y = b_ref[...] + keep * own_ref[:, wide : wide + 128]
    for n in range(4):
        y += jnp.dot(f_ref[n], others[n][:, wide : wide + 128], precision=highest, preferred_element_type=f32)
    if radius == REACH:
        out_ref[...] = held[5]
        y_ref[...] = y
    else:
        out = tuple((a, b) for a in range(-radius, radius + 1) for b in range(-radius, radius + 1) if abs(a) + abs(b) <= radius)
        for i, (a, b) in enumerate(out):
            at = (b + REACH) * K
            out_ref[:, i * K : i * K + K] = held[5, a + REACH, :, at : at + K]
        if len(out) % 2:
            out_ref[:, len(out) * K : len(out) * K + K] = jnp.zeros((K, K), f32)
        wide_out = -(-len(out) // 2) * 2 * K
        out_ref[:, wide_out : wide_out + 128] = y


def expand_into(w_ref, y_ref, store):
    width = 4
    step = 16

    def layers(xb, _):
        def some(kb, sums):
            for ki in range(step):
                k = kb * step + ki
                y = jnp.broadcast_to(y_ref[pl.ds(k, 1)], (CY, 128))
                y = jnp.concatenate([y] * (NZ // 128), axis=1)
                sums = tuple(
                    sums[i] + y * w_ref[k, xb * width + i].astype(f32) for i in range(width)
                )
            return sums

        sums = lax.fori_loop(0, K // step, some, tuple(jnp.zeros((CY, NZ), f32) for _ in range(width)))
        for i in range(width):
            store(xb * width + i, sums[i])
        return 0

    lax.fori_loop(0, CX // width, layers, 0)


def project_row(w_ref, v_ref, gp):
    half = CX // 2
    step = 8
    for h in range(2):
        values = [v_ref[h * half + i].astype(bf16).astype(f32) for i in range(half)]

        def some(kb, _, h=h, values=values):
            for ki in range(step):
                k = kb * step + ki
                total = values[0] * w_ref[k, h * half].astype(f32)
                for i in range(1, half):
                    total += values[i] * w_ref[k, h * half + i].astype(f32)
                part = total[:, :128] + total[:, 128:256] + total[:, 256:]
                if h == 0:
                    gp[k] = part
                else:
                    gp[k] += part
            return 0

        lax.fori_loop(0, K // step, some, 0)
    lanes = jnp.sum(gp[...], axis=1)
    return lax.dot_general(
        jnp.ones((8, 128), f32), lanes, (((1,), (1,)), ((), ())), precision=highest, preferred_element_type=f32
    )


def apply_layer(v, x, fx_ref, fy_ref, fz_ref, dg_ref):
    here = v[x]
    fy = fy_ref[x]
    fz = fz_ref[x]
    out = dg_ref[x] * here - fx_ref[x - 1] * v[x - 1] - fx_ref[x] * v[x + 1]
    return out - up(fy * here) - fy * down(here) - back(fz * here) - fz * fore(here)


def fill(ext, own, xm, xp, ym, yp):
    ext[...] = jnp.zeros_like(ext)
    deep = xm.shape[0]
    ext[2 : 2 + CX, Y0 : Y0 + CY] = own[...]
    ext[2 - deep : 2, Y0 : Y0 + CY] = xm[...]
    ext[2 + CX : 2 + CX + deep, Y0 : Y0 + CY] = xp[...]
    if deep == 2:
        for j in range(2):
            ext[:, Y0 - 2 + j] = ym[j]
            ext[:, Y0 + CY + j] = yp[j]
    else:
        ext[2 : 2 + CX, Y0 - 1] = ym[...]
        ext[2 : 2 + CX, Y0 + CY] = yp[...]


def solve_rows(where, got, r_ref, got_ref):
    got_ref[...] = got[:, :128]
    r = where[0]
    c = where[1]
    rows = where[2]
    cols = where[3]
    lane = lax.broadcasted_iota(jnp.int32, (1, 128), 1)
    total = jnp.zeros((K, 128), f32)
    for a in range(-REACH, REACH + 1):
        at = jnp.clip(r + a, 0, rows - 1) * cols
        for q in range(BLOCKS // 2):
            b = 2 * q - REACH
            if min(abs(b), abs(b + 1)) + abs(a) > REACH:
                continue
            first = got_ref[pl.ds(at + jnp.clip(c + b, 0, cols - 1), 1)]
            second = got_ref[pl.ds(at + jnp.clip(c + b + 1, 0, cols - 1), 1)]
            total += r_ref[a + REACH, :, q * 128 : q * 128 + 128] * jnp.where(lane < K, first, second)
    return jnp.sum(total, axis=1, keepdims=True)


def rounded(y):
    return jnp.broadcast_to(y, (K, 128)).astype(bf16).astype(f32)


def fold(parts):
    parts = parts[:, :128] + parts[:, 128:256] + parts[:, 256:]
    return jnp.sum(parts, axis=0, keepdims=True)


def first_kernel(f_ref, b_ref, y_in, nxm, nxp, nym, nyp, w_ref, x_ref, yb):
    y = b_ref[...] + keep * y_in[...]
    for n, other in enumerate((nxm, nxp, nym, nyp)):
        y += jnp.dot(f_ref[n], other[...], precision=highest, preferred_element_type=f32)
    yb[...] = y.astype(bf16).astype(f32)

    def store(x, v):
        x_ref[x] = v

    expand_into(w_ref, yb, store)


def residual_kernel(
    x_ref, xm, xp, ym, yp, rhs_ref, rxm, rxp, rym, ryp, fx_ref, fy_ref, fz_ref, dg_ref, inv_ref, w_ref,
    r_ref, pay_ref, ext, mid, field, gp,
):
    fill(ext, x_ref, xm, xp, ym, yp)
    fill(mid, rhs_ref, rxm, rxp, rym, ryp)
    for x in range(1, EX - 1):
        mid[x] = mid[x] - apply_layer(ext, x, fx_ref, fy_ref, fz_ref, dg_ref)
    r_ref[...] = mid[2 : 2 + CX, Y0 : Y0 + CY]
    for x in range(CX):
        field[x] = apply_layer(mid, x + 2, fx_ref, fy_ref, fz_ref, dg_ref)[Y0 : Y0 + CY]
    g = project_row(w_ref, field, gp)
    b = relax * jnp.dot(g, inv_ref[...], precision=highest, preferred_element_type=f32)
    pay_ref[...] = jnp.concatenate([b[:1], b[:1]], axis=1)


def direction_kernel(where, got_ref, rr_ref, w_ref, base_ref, d_ref, yb, lines):
    yb[...] = rounded(solve_rows(where, got_ref, rr_ref, lines))

    def store(x, v):
        d_ref[x] = base_ref[x] - v

    expand_into(w_ref, yb, store)


def image_kernel(
    d_ref, xm, xp, ym, yp, r_ref, fx_ref, fy_ref, fz_ref, dg_ref, inv_ref, w_ref,
    i_ref, pay_ref, ext, mid, field, gp,
):
    fill(ext, d_ref, xm, xp, ym, yp)
    for x in range(1, EX - 1):
        mid[x] = apply_layer(ext, x, fx_ref, fy_ref, fz_ref, dg_ref)
    mid[0] = jnp.zeros((EY, NZ), f32)
    mid[EX - 1] = jnp.zeros((EY, NZ), f32)
    i_ref[...] = mid[2 : 2 + CX, Y0 : Y0 + CY]
    rr = jnp.zeros((CY, NZ), f32)
    dw = jnp.zeros((CY, NZ), f32)
    for x in range(CX):
        field[x] = apply_layer(mid, x + 2, fx_ref, fy_ref, fz_ref, dg_ref)[Y0 : Y0 + CY]
        rr += r_ref[x] * r_ref[x]
        dw += d_ref[x] * i_ref[x]
    g = project_row(w_ref, field, gp)
    b = relax * jnp.dot(g, inv_ref[...], precision=highest, preferred_element_type=f32)
    pay_ref[:, :K] = b[:1]
    pay_ref[:, K : 2 * K] = b[:1]
    pay_ref[:, 128:256] = fold(rr)
    pay_ref[:, 256:384] = fold(dw)


def total_of(got_ref, at):
    return jnp.sum(jnp.sum(got_ref[:, at : at + 128], axis=0, keepdims=True), axis=1, keepdims=True)


def last_kernel(
    e_ref, xm, xp, ym, yp, got_ref, r_ref, d_ref, i_ref, fx_ref, fy_ref, fz_ref, dg_ref,
    r1_ref, z_ref, az_ref, pay_ref, ext,
):
    alpha = total_of(got_ref, 128) / total_of(got_ref, 256)
    fill(ext, e_ref, xm, xp, ym, yp)
    rr = jnp.zeros((CY, NZ), f32)
    zi = jnp.zeros((CY, NZ), f32)
    za = jnp.zeros((CY, NZ), f32)
    for x in range(CX):
        image = i_ref[x]
        az = image - alpha * apply_layer(ext, x + 2, fx_ref, fy_ref, fz_ref, dg_ref)[Y0 : Y0 + CY]
        z = d_ref[x] - alpha * e_ref[x]
        r1 = r_ref[x] - alpha * image
        r1_ref[x] = r1
        z_ref[x] = z
        az_ref[x] = az
        rr += r1 * r1
        zi += z * image
        za += z * az
    pay_ref[:, 0:128] = fold(rr)
    pay_ref[:, 128:256] = fold(zi)
    pay_ref[:, 256:384] = fold(za)


def finish_kernel(got_ref, fin_ref, x_ref, d_ref, i_ref, r1_ref, z_ref, az_ref, sol_ref, res_ref):
    rr0 = total_of(got_ref, 128)
    dw0 = total_of(got_ref, 256)
    rr1 = total_of(fin_ref, 0)
    zi = total_of(fin_ref, 128)
    za = total_of(fin_ref, 256)
    alpha0 = rr0 / dw0
    beta = rr1 / rr0
    alpha1 = rr1 / (beta * beta * dw0 + 2.0 * beta * zi + za)
    for x in range(CX):
        d = d_ref[x]
        sol_ref[x] = x_ref[x] + alpha0 * d + alpha1 * (beta * d + z_ref[x])
        res_ref[x] = r1_ref[x] - alpha1 * (beta * i_ref[x] + az_ref[x])


def lateral(x):
    return (ring(x, "row", 1), ring(x, "row", -1), ring(x, "col", 1), ring(x, "col", -1))


def halo_deep(field, last):
    xm = ring(field[CX - 2 :], "row", 1)
    xp = ring(field[:2], "row", -1)
    low = jnp.concatenate([xm[:, :2], field[:, :2], xp[:, :2]], axis=0).transpose(1, 0, 2)
    high = jnp.concatenate([xm[:, CY - 2 :], field[:, CY - 2 :], xp[:, CY - 2 :]], axis=0).transpose(1, 0, 2)
    return (xm, xp, ring(high, "col", 1), ring(low, "col", -1))


def halo_edge(field):
    return (
        ring(field[CX - 1 :], "row", 1),
        ring(field[:1], "row", -1),
        ring(field[:, CY - 1], "col", 1),
        ring(field[:, 0], "col", -1),
    )


def body(rhs, storage, class_id, table, basis):
    where = jnp.stack(
        [lax.axis_index("row"), lax.axis_index("col"), lax.axis_size("row"), lax.axis_size("col")]
    ).astype(jnp.int32)
    field = (CX, CY, NZ)
    wide = (EX, EY, NZ)
    vm = pltpu.VMEM

    ids = halo_deep(class_id, TILES)
    stor = halo_edge(storage)
    rhs_halo = halo_edge(rhs)
    ofx, ofy = call(faces_kernel, [((2, CY, K, NZ), bf16), ((2, CX, K, NZ), bf16)], (basis,))
    near = (ring(ofx[1], "row", 1), ring(ofx[0], "row", -1), ring(ofy[1], "col", 1), ring(ofy[0], "col", -1))
    gram, proj = call(
        galerkin_kernel,
        [((K, K), f32), ((K, 128), f32)],
        (table, basis, class_id, storage, rhs),
        [vm((4,) + field, f32), vm((4, K, CY, NZ), bf16), vm((K * CY, K * CY), f32), vm((K, 8, 128), f32)],
        smem=1,
        flops=20000000,
    )
    fx, fy, fz, dg, inv, b = call(
        coef_kernel,
        [(wide, f32)] * 4 + [((K, K), f32), ((K, 128), f32)],
        (where, table, class_id) + ids + (storage,) + stor + (ofx, ofy, gram, proj),
        [vm(wide, f32), vm(wide, f32)],
        smem=2,
    )
    coefs = (fx, fy, fz, dg)
    minus_f, m1 = call(
        couple_kernel, [((4, K, K), f32), ((K, 8 * K), f32)], (fx, fy, inv, b, ofx, ofy) + near
    )
    held = [vm((6, 2 * REACH + 1, K, BLOCKS * K), f32)]
    m2, _ = call(
        functools.partial(spread_kernel, R1_BLOCKS, 2, None),
        [((K, 16 * K), f32), ((8, 128), f32)],
        (minus_f, b, m1) + lateral(m1),
        held,
    )
    rows, y2 = call(
        functools.partial(spread_kernel, R2_BLOCKS, 3, None),
        [((2 * REACH + 1, K, BLOCKS * K), f32), ((K, 128), f32)],
        (minus_f, b, m2) + lateral(m2),
        held,
    )
    yb = [vm((K, 128), f32)]
    line = yb + [vm((lax.axis_size(("row", "col")), 128), f32)]
    (x0,) = call(first_kernel, [(field, f32)], (minus_f, b, y2) + lateral(y2) + (basis,), yb)
    work = [vm(wide, f32), vm(wide, f32), vm(field, f32), vm((K, 8, 128), f32)]
    r0, pay = call(
        residual_kernel,
        [(field, f32), ((1, 128), f32)],
        (x0,) + halo_deep(x0, NZ) + (rhs,) + rhs_halo + coefs + (inv, basis),
        work,
    )
    (d0,) = call(direction_kernel, [(field, f32)], (where, gather(pay), rows, basis, r0), line, smem=1)
    image, pay = call(
        image_kernel,
        [(field, f32), ((1, 384), f32)],
        (d0,) + halo_deep(d0, NZ) + (r0,) + coefs + (inv, basis),
        work,
    )
    got = gather(pay)
    (e0,) = call(direction_kernel, [(field, f32)], (where, got, rows, basis, image), line, smem=1)
    r1, z, az, pay = call(
        last_kernel,
        [(field, f32)] * 3 + [((1, 384), f32)],
        (e0,) + halo_edge(e0) + (got, r0, d0, image) + coefs,
        [vm(wide, f32)],
    )
    return tuple(
        call(finish_kernel, [(field, f32)] * 2, (got, gather(pay), x0, d0, image, r1, z, az))
    )


def solution(mesh):
    placed = (
        P("row", "col", None),
        P("row", "col", None),
        P("row", "col", None),
        P(),
        P(None, "row", "col", None),
    )
    return jax.shard_map(
        body,
        mesh=mesh,
        in_specs=placed,
        out_specs=(P("row", "col", None), P("row", "col", None)),
        check_vma=False,
    )
```
